32 devices in a mesh: dp: 8 (over y, x, core), expert: 4 (over z).
Axes of the slice: x: 2, y: 2, z: 4, core: 2. Of those that a mesh axis runs over, the one named last changes fastest.
Arguments:
- out_grad: bfloat16 [512, 4096], P('expert', 'dp'), may hold values from -6 to 6
- logits: float32 [512, 16], P('expert'), may hold values from -12 to 12
- routes: int32 [512, 8], P('expert'), may hold values from 0 to 15, all different within a row; in each aligned block of 128 rows (0 to 127, 128 to 255, ...) at most 96 rows name the same one
- hidden: bfloat16 [16, 384, 1536], P('expert'), may hold values from -6 to 6
- w_down: bfloat16 [16, 1536, 4096], P('expert', None, 'dp'), may hold values from -0.15625 to 0.15625
Outputs:
- grad_down: bfloat16 [16, 1536, 4096], P('expert', None, 'dp')
- grad_hidden: bfloat16 [384, 16, 1536], P('dp', 'expert')
- grad_logits: float32 [512, 16], P('expert')
The draws below stay inside these ranges and needn't reach their ends.
Inputs may be any that keep to these rules, and one draw needn't show every extreme that they name: `routes`: within the 128 rows of one device no expert is named more than 96 times, a bound that some block reaches; the experts of one row differ.
All inputs are finite; a program needn't handle non-finite values.
Results may differ from the reference program's by a relative error of at most 0.0057.
Values may be sent and summed in bfloat16 or wider, within the bound.
A program may use at most 64 MiB of HBM per device.

```python
import math
import jax
import jax.numpy as jnp
import numpy as np
from jax import lax

D = 4096
F = 1536
TOP = 8
TOK_DEV = 128
EXPERTS = 16
TOKENS = 512
CAP = 96
SLOTS = 384
N_EXPERT = 4


def block_levels(rng, shape, split, smallest, largest):
    def one(dim, shards_of):
        draws = jax.random.uniform(jax.random.fold_in(jax.random.fold_in(rng, 6), dim), (shards_of,), jnp.float32, smallest / len(split), largest / len(split))
        return jnp.repeat(jnp.exp(draws), shape[dim] // shards_of).reshape((-1,) + (1,) * (len(shape) - dim - 1))

    factor_of = one(*split[0])
    for cut in split[1:]:
        factor_of = factor_of * one(*cut)
    return factor_of


def assign_block(rng, own, number, rows, number_of, top, limit, slope):
    sequence = jax.random.permutation(rng, number_of)
    heavy_load, common = shares(number_of, rows * top, limit, slope, True), shares(number_of, rows * top, limit, slope, False)
    places = jnp.arange(number_of)

    def named(sizes, turn):
        used = int((sizes > 0).sum())
        fixed = max(1, used // 4)
        passed = fixed + (places - fixed + turn * (used - fixed)) % max(1, number_of - fixed)
        return jnp.zeros((number_of,), jnp.int32).at[sequence[jnp.where(places < fixed, places, passed)]].set(jnp.asarray(sizes, jnp.int32))

    sizes = jnp.where(number % 4 == 0, named(heavy_load, number // 4), named(common, number - number // 4 - 1))
    mixed = jax.random.permutation(jax.random.fold_in(own, 3), number_of)
    donor, sink = mixed[0:number_of // 2 * 2:2], mixed[1:number_of // 2 * 2:2]
    room = jnp.minimum(sizes[donor] - 1, limit - sizes[sink]) // 2
    room = jnp.where((donor == sequence[0]) | (sink == sequence[0]) | (sizes[sink] == 0), 0, jnp.maximum(room, 0))
    passed = jax.random.randint(jax.random.fold_in(own, 4), (number_of // 2,), 0, 1 << 20) % (room + 1)
    sizes = sizes.at[donor].add(-passed).at[sink].add(passed)
    labels = jnp.searchsorted(jnp.cumsum(sizes), jnp.arange(rows * top), side="right").astype(jnp.int32)
    listing = labels.reshape(top, rows).T
    listing = listing[jax.random.permutation(jax.random.fold_in(own, 1), rows)]
    turn = jax.random.randint(jax.random.fold_in(own, 2), (rows, 1), 0, top)
    return jnp.take_along_axis(listing, (jnp.arange(top)[None, :] + turn) % top, axis=1)


def shares(amount, total, reach, skew, full):
    portions = [(1 << 20) // math.isqrt(standing ** skew) + 1 for standing in range(1, amount + 1)]
    largest = reach if full else min(reach, max(-(-total // amount), total * portions[0] // sum(portions)))
    least = 1 if total - largest >= amount - 1 else 0
    counts, surplus = [largest] + [least] * (amount - 1), total - largest - least * (amount - 1)
    while surplus > 0:
        candidates = [i for i in range(1, amount) if counts[i] < largest] or [i for i in range(1, amount) if counts[i] < reach]
        whole, remaining = sum([portions[i] for i in candidates]), surplus
        for i in candidates:
            more = min(reach - counts[i], max(1, remaining * portions[i] // whole), surplus)
            counts[i] = counts[i] + more
            surplus = surplus - more
    return np.array(counts)


def centred(stream_key, dims, deviation, limit, split=(), kind=jnp.bfloat16):
    level = block_levels(stream_key, dims, split, -0.22, 0.18) if split else 1.0
    drawn = jax.random.normal(stream_key, dims, jnp.float32) * deviation * level
    return jnp.minimum(jnp.maximum(drawn, -limit), limit).astype(kind)


def setup_inputs(seed: int = 0) -> dict:
    key_list = jax.random.split(jax.random.key(seed), 6)
    out_grad = centred(key_list[0], (TOKENS, D), 1.0, 6.0, ((0, 4), (1, 8)))
    logits = centred(key_list[1], (TOKENS, EXPERTS), 2.0, 12.0, ((0, 4),), jnp.float32)
    routes_keys = jax.random.split(jax.random.fold_in(key_list[2], 1), TOKENS // TOK_DEV)
    routes_turns = jax.random.permutation(jax.random.fold_in(key_list[2], 3), TOKENS // TOK_DEV)
    routes = jax.vmap(lambda own, number: assign_block(jax.random.fold_in(key_list[2], 2), own, number, TOK_DEV, EXPERTS, TOP, CAP, 2))(routes_keys, routes_turns).reshape((TOKENS, TOP))
    hidden = centred(key_list[3], (EXPERTS, SLOTS, F), 1.0, 6.0, ((0, 4),))
    w_down = centred(key_list[4], (EXPERTS, F, D), F ** -0.5, 0.15625, ((0, 4), (2, 8)))
    return {"out_grad": out_grad, "logits": logits, "routes": routes, "hidden": hidden, "w_down": w_down}


def expert_terms(items):
    hid, weight, disp, wts = items
    scaled = (wts[:, None] * disp.astype(jnp.float32)).astype(jnp.bfloat16)
    grad_w = jnp.dot(hid.T, scaled, preferred_element_type=jnp.float32).astype(jnp.bfloat16)
    inner = jnp.dot(disp, weight.T, preferred_element_type=jnp.float32)
    grad_h = (wts[:, None] * inner).astype(jnp.bfloat16)
    dslot = jnp.sum(hid.astype(jnp.float32) * inner, axis=1)
    return grad_w, grad_h, dslot


def reference(out_grad, logits, routes, hidden, w_down):
    probs = jax.nn.softmax(logits, axis=-1)
    sel = jnp.take_along_axis(probs, routes, axis=1)
    wsum = jnp.sum(sel, axis=1)
    comb = sel / wsum[:, None]
    comb_b = comb.astype(jnp.bfloat16)
    onehot = (routes[:, :, None] == jnp.arange(EXPERTS, dtype=jnp.int32)[None, None, :]).astype(jnp.int32)
    blocks = onehot.reshape(N_EXPERT, TOK_DEV * TOP, EXPERTS)
    before = jnp.cumsum(blocks, axis=1) - blocks
    rank = jnp.sum(before * blocks, axis=2).reshape(TOKENS, TOP)
    source = (jnp.arange(TOKENS, dtype=jnp.int32) // TOK_DEV)[:, None]
    slot = (source * CAP + rank).astype(jnp.int32)
    rows = jnp.broadcast_to(out_grad[:, None, :], (TOKENS, TOP, D))
    dispatched = jnp.zeros((EXPERTS, SLOTS, D), jnp.bfloat16).at[routes, slot].set(rows)
    weights = jnp.zeros((EXPERTS, SLOTS), jnp.float32).at[routes, slot].set(comb_b.astype(jnp.float32))
    grad_down, grad_h, dslot = lax.map(expert_terms, (hidden, w_down, dispatched, weights))
    grad_hidden = jnp.transpose(grad_h, (1, 0, 2))
    dcomb = dslot[routes, slot]
    dsel = (dcomb - jnp.sum(comb * dcomb, axis=1, keepdims=True)) / wsum[:, None]
    spread = jnp.sum(onehot.astype(jnp.float32) * dsel[:, :, None], axis=1)
    grad_logits = probs * (spread - jnp.sum(sel * dsel, axis=1, keepdims=True))
    return grad_down, grad_hidden, grad_logits
```

```python
import functools

import jax
import jax.numpy as jnp
from jax import lax
from jax.experimental import pallas as pl
from jax.experimental.pallas import tpu as pltpu
from jax.sharding import PartitionSpec as P

MESH = pl.DeviceIdType.MESH
F32, BF16 = jnp.float32, jnp.bfloat16
GROUP = 8


def bit_of(value, b):
    return lax.rem(value // (1 << b), 2) if not isinstance(value, int) else (value >> b) & 1


def flipped(value, b):
    return value + (1 << b) * (1 - 2 * bit_of(value, b))


def stream_bits(levels, expert):
    rest = list(range(1, levels))
    return [0] + (rest if expert % 2 == 0 else rest[::-1])


def relative(position, bits):
    levels = len(bits)
    return sum(((position >> (levels - 1 - k)) & 1) << b for k, b in enumerate(bits))


def kernel(
    nz, nd, own, pad, cap, experts, ft,
    og_ref, lt_ref, rt_ref, hid_hbm, w_hbm,
    gh_ref, gl_ref, scaled_ref,
    w, hid, og, meta, gmeta, onehot, disp, wcol, acc, snd, rcv, dsl, dc, dcr, ret,
    load_sem, og_s, og_r, mt_s, mt_r, rs_s, rs_r, ar_s, ar_r, z_s, z_r,
):
    me_d, me_z = lax.axis_index("dp"), lax.axis_index("expert")
    levels = nd.bit_length() - 1
    rows = nd * pad
    half = rows // 2
    tok = og_ref.shape[0]
    hidden_units = w.shape[1]

    loads = []
    for e in range(experts):
        pair = (
            pltpu.make_async_copy(w_hbm.at[e], w.at[e], load_sem.at[2 * e]),
            pltpu.make_async_copy(hid_hbm.at[e], hid.at[e], load_sem.at[2 * e + 1]),
        )
        for copy in pair:
            copy.start()
        loads.append(pair)

    barrier = pltpu.get_barrier_semaphore()
    for k in range(1, nz):
        pl.semaphore_signal(barrier, inc=1, device_id=(me_d, lax.rem(me_z + k, nz)), device_id_type=MESH)
    for b in range(levels):
        pl.semaphore_signal(barrier, inc=1, device_id=(flipped(me_d, b), me_z), device_id_type=MESH)

    lt = lt_ref[...]
    row = lax.broadcasted_iota(jnp.int32, lt.shape, 0)
    local = lax.rem(row, GROUP)
    eid = jnp.where(local < experts, (row // GROUP) * experts + local, -1)
    top = rt_ref.shape[0]
    chosen = jnp.zeros(lt.shape, F32)
    for k in range(top):
        chosen = jnp.where(rt_ref[k : k + 1, :] == eid, 1.0, chosen)
    raised = jnp.exp(lt - jnp.max(lt, axis=0, keepdims=True))
    probs = raised / jnp.sum(raised, axis=0, keepdims=True)
    sel = probs * chosen
    wsum = jnp.sum(sel, axis=0, keepdims=True)
    comb = sel / wsum
    t2 = lax.broadcasted_iota(jnp.int32, (tok, tok), 0)
    t1 = lax.broadcasted_iota(jnp.int32, (tok, tok), 1)
    earlier = jnp.where(t2 < t1, 1.0, 0.0).astype(BF16)
    rank = jnp.dot(chosen.astype(BF16), earlier, preferred_element_type=F32)
    place = jnp.where(chosen > 0.5, rank, -1.0)
    for z in range(nz):
        part = slice(z * GROUP, (z + 1) * GROUP)
        meta[z] = jnp.concatenate([place[part], comb[part]], axis=0).astype(BF16)

    pl.semaphore_wait(barrier, nz - 1 + levels)
    copies = []
    for k in range(1, nz):
        to = lax.rem(me_z + k, nz)
        copies.append(pltpu.make_async_remote_copy(
            src_ref=og_ref, dst_ref=og.at[me_z], send_sem=og_s.at[k - 1], recv_sem=og_r.at[k - 1],
            device_id=(me_d, to), device_id_type=MESH))
        copies.append(pltpu.make_async_remote_copy(
            src_ref=meta.at[to], dst_ref=gmeta.at[me_z], send_sem=mt_s.at[k - 1], recv_sem=mt_r.at[k - 1],
            device_id=(me_d, to), device_id_type=MESH))
    for copy in copies:
        copy.start()
    og[me_z] = og_ref[...]
    gmeta[me_z] = meta[me_z]

    at = lax.broadcasted_iota(jnp.int32, (rows, tok), 0)
    position, inside = at // pad, lax.rem(at, pad)
    slot_at = []
    for stream in range(2):
        bits = stream_bits(levels, stream)
        owner = jnp.zeros_like(at)
        for k, b in enumerate(bits):
            differs = lax.rem(position // (1 << (levels - 1 - k)), 2)
            owner = owner + (1 << b) * lax.rem(differs + bit_of(me_d, b), 2)
        slot_at.append(jnp.where(inside < own, owner * own + inside, -7).astype(F32))

    def owner_of(p, bits):
        r = relative(p, bits)
        return sum((1 << b) * lax.rem(bit_of(r, b) + bit_of(me_d, b), 2) for b in range(levels))

    for copy in copies:
        copy.wait()

    def rs_copy(e, level):
        bits = stream_bits(levels, e)
        size = rows >> (level + 1)
        start = rows - (rows >> level)
        return pltpu.make_async_remote_copy(
            src_ref=snd.at[e, pl.ds(start, size)], dst_ref=rcv.at[e, pl.ds(start, size)],
            send_sem=rs_s.at[e * levels + level], recv_sem=rs_r.at[e * levels + level],
            device_id=(flipped(me_d, bits[level]), me_z), device_id_type=MESH)

    def compute(e):
        bits = stream_bits(levels, e)
        slots = slot_at[e % 2]
        wcol[e] = jnp.zeros((rows, tok), F32)

        def dispatch(s):
            told = gmeta[s].astype(F32)
            place_row, comb_row = told[e : e + 1], told[GROUP + e : GROUP + e + 1]
            offset = s * cap if isinstance(s, int) else (s * cap).astype(F32)
            absolute = jnp.where(place_row >= 0.0, place_row + offset, -1.0)
            hit = slots == absolute
            lanes = pl.ds(s * tok if isinstance(s, int) else pl.multiple_of(s * tok, tok), tok)
            onehot[e, :, lanes] = jnp.where(hit, 1.0, 0.0).astype(BF16)
            wcol[e] += jnp.where(hit, comb_row, 0.0)

        if nz <= 8:
            for s in range(nz):
                dispatch(s)
        else:
            @pl.loop(0, nz)
            def _(s):
                dispatch(s)

        weight = jnp.sum(wcol[e], axis=1, keepdims=True)
        wcol[e] = jnp.broadcast_to(weight, (rows, tok))
        cols = og.shape[2]
        d = jnp.dot(onehot[e], og[...].reshape(nz * tok, cols), preferred_element_type=F32)
        disp[...] = d.astype(BF16)
        scaled = (weight * d).astype(BF16)
        for p in range(nd):
            scaled_ref[e, owner_of(p, bits)] = scaled[p * pad : (p + 1) * pad]
        for copy in loads[e]:
            copy.wait()
        dsl[...] = jnp.zeros(dsl.shape, F32)

        @pl.loop(0, hidden_units // ft)
        def _(i):
            part = pl.ds(pl.multiple_of(i * ft, ft), ft)
            u = lax.dot_general(disp[...], w[e, part, :], (((1,), (1,)), ((), ())), preferred_element_type=F32)
            acc[e, :, part] = u[:half]
            snd[e, 0:half, part] = u[half:].astype(BF16)
            for p in range(nd):
                prod = u[p * pad : (p + 1) * pad] * hid[e, owner_of(p, bits), :, part].astype(F32)
                total = prod[:, 0:128]
                for c in range(128, ft, 128):
                    total = total + prod[:, c : c + 128]
                dsl[p * pad : (p + 1) * pad, :] += total

        rs_copy(e, 0).start()
        line = jnp.sum(jnp.transpose(dsl[...]), axis=0, keepdims=True)
        high = line.astype(BF16).astype(F32)
        mid = (line - high).astype(BF16).astype(F32)
        low = line - high - mid
        which = lax.broadcasted_iota(jnp.int32, (16, rows), 0)
        three = jnp.where(which == 0, high, jnp.where(which == 1, mid, jnp.where(which == 2, low, 0.0))).astype(BF16)
        back = jnp.dot(three, onehot[e], preferred_element_type=F32)
        back = jnp.sum(back, axis=0, keepdims=True)
        for s in range(nz):
            dc[0, s, e : e + 1, :] = back[:, s * tok : (s + 1) * tok]

    def advance(e, level):
        copy = rs_copy(e, level)
        copy.wait()
        size = rows >> (level + 1)
        start = rows - (rows >> level)
        if level < levels - 1:
            keep = size // 2
            snd[e, start + size : start + size + keep] = (
                acc[e, keep:size] + rcv[e, start + keep : start + size].astype(F32)).astype(BF16)
            rs_copy(e, level + 1).start()
            acc[e, 0:keep] += rcv[e, start : start + keep].astype(F32)
        else:
            total = acc[e, 0:size] + rcv[e, start : start + size].astype(F32)
            gh_ref[e] = (wcol[e, 0:size, 0:1] * total).astype(BF16)

    def ar_copy(level):
        return pltpu.make_async_remote_copy(
            src_ref=dc.at[level], dst_ref=dcr.at[level], send_sem=ar_s.at[level], recv_sem=ar_r.at[level],
            device_id=(flipped(me_d, level), me_z), device_id_type=MESH)

    dc[0] = jnp.zeros(dc.shape[1:], F32)
    compute(0)
    for e in range(1, experts):
        compute(e)
        advance(e - 1, 0)

    def ar_step(level):
        ar_copy(level).wait()
        dc[level + 1] = dc[level] + dcr[level]

    ar_copy(0).start()
    advance(experts - 1, 0)
    for level in range(levels):
        ar_step(level)
        if level + 1 < levels:
            ar_copy(level + 1).start()
    returns = []
    for k in range(1, nz):
        to = lax.rem(me_z + k, nz)
        returns.append(pltpu.make_async_remote_copy(
            src_ref=dc.at[levels, to], dst_ref=ret.at[me_z], send_sem=z_s.at[k - 1], recv_sem=z_r.at[k - 1],
            device_id=(me_d, to), device_id_type=MESH))
    for copy in returns:
        copy.start()
    ret[me_z] = dc[levels, me_z]

    for level in range(1, levels):
        for e in range(experts):
            advance(e, level)

    for copy in returns:
        copy.wait()
    dcomb = ret[...].reshape(nz * GROUP, tok)
    dsel = (dcomb - jnp.sum(comb * dcomb, axis=0, keepdims=True)) / wsum
    spread = jnp.where(chosen > 0.5, dsel, 0.0)
    gl_ref[...] = probs * (spread - jnp.sum(sel * spread, axis=0, keepdims=True))


def per_device(out_grad, logits, routes, hidden, w_down):
    tok, cols = out_grad.shape
    experts, slot_count, units = hidden.shape
    nz, nd = lax.axis_size("expert"), lax.axis_size("dp")
    cap, own = slot_count // nz, slot_count // nd
    pad = -(-own // 16) * 16
    rows, levels = nd * pad, nd.bit_length() - 1
    ft = next(f for f in (512, 384, 256, 128) if units % f == 0)

    lt = logits.T.reshape(nz, experts, tok)
    lt = jnp.pad(lt, ((0, 0), (0, GROUP - experts), (0, 0)), constant_values=-1e30).reshape(nz * GROUP, tok)
    hid = hidden.reshape(experts, nd, own, units)
    if pad != own:
        hid = jnp.pad(hid, ((0, 0), (0, 0), (0, pad - own), (0, 0)))
    vmem, hbm = pl.BlockSpec(memory_space=pltpu.VMEM), pl.BlockSpec(memory_space=pl.ANY)
    dma = lambda n: pltpu.SemaphoreType.DMA((n,))
    gh, gl, scaled = pl.pallas_call(
        functools.partial(kernel, nz, nd, own, pad, cap, experts, ft),
        out_shape=(
            jax.ShapeDtypeStruct((experts, pad, units), BF16),
            jax.ShapeDtypeStruct((nz * GROUP, tok), F32),
            jax.ShapeDtypeStruct((experts, nd, pad, cols), BF16),
        ),
        in_specs=[vmem, vmem, vmem, hbm, hbm],
        out_specs=(vmem, vmem, vmem),
        scratch_shapes=[
            pltpu.VMEM((experts, units, cols), BF16),
            pltpu.VMEM((experts, nd, pad, units), BF16),
            pltpu.VMEM((nz, tok, cols), BF16),
            pltpu.VMEM((nz, 2 * GROUP, tok), BF16),
            pltpu.VMEM((nz, 2 * GROUP, tok), BF16),
            pltpu.VMEM((experts, rows, nz * tok), BF16),
            pltpu.VMEM((rows, cols), BF16),
            pltpu.VMEM((experts, rows, tok), F32),
            pltpu.VMEM((experts, rows // 2, units), F32),
            pltpu.VMEM((experts, rows, units), BF16),
            pltpu.VMEM((experts, rows, units), BF16),
            pltpu.VMEM((rows, 128), F32),
            pltpu.VMEM((levels + 1, nz, GROUP, tok), F32),
            pltpu.VMEM((levels, nz, GROUP, tok), F32),
            pltpu.VMEM((nz, GROUP, tok), F32),
            dma(2 * experts), dma(nz - 1), dma(nz - 1), dma(nz - 1), dma(nz - 1),
            dma(experts * levels), dma(experts * levels), dma(levels), dma(levels), dma(nz - 1), dma(nz - 1),
        ],
        compiler_params=pltpu.CompilerParams(
            collective_id=0, has_side_effects=True, vmem_limit_bytes=60 * 1024 * 1024),
    )(out_grad, lt, routes.T, hid, w_down)

    grad_down = jnp.einsum(
        "ecsf,ecsd->efd", hid, scaled, preferred_element_type=F32) if pad != own else jnp.einsum(
        "esf,esd->efd", hidden, scaled.reshape(experts, slot_count, cols), preferred_element_type=F32)
    grad_hidden = jnp.transpose(gh[:, :own], (1, 0, 2))
    grad_logits = gl.reshape(nz, GROUP, tok)[:, :experts].reshape(nz * experts, tok).T
    return grad_down.astype(BF16), grad_hidden, grad_logits


def solution(mesh):
    return jax.shard_map(
        per_device,
        mesh=mesh,
        in_specs=(
            P("expert", "dp"),
            P("expert", None),
            P("expert", None),
            P("expert", None, None),
            P("expert", None, "dp"),
        ),
        out_specs=(P("expert", None, "dp"), P("dp", "expert", None), P("expert", None)),
        check_vma=False,
    )
```

```python
import functools

import jax
import jax.numpy as jnp
from jax import lax
from jax.experimental import pallas as pl
from jax.experimental.pallas import tpu as pltpu
from jax.sharding import PartitionSpec as P

MESH = pl.DeviceIdType.MESH
F32, BF16 = jnp.float32, jnp.bfloat16
GROUP = 8


def bit_of(value, b):
    return lax.rem(value // (1 << b), 2) if not isinstance(value, int) else (value >> b) & 1


def flipped(value, b):
    return value + (1 << b) * (1 - 2 * bit_of(value, b))


def stream_bits(levels, expert):
    rest = list(range(1, levels))
    return [0] + (rest if expert % 2 == 0 else rest[::-1])


def relative(position, bits):
    levels = len(bits)
    return sum(((position >> (levels - 1 - k)) & 1) << b for k, b in enumerate(bits))


def kernel(
    nz, nd, own, pad, cap, experts, ft,
    og_ref, lt_ref, rt_ref, hid_hbm, w_hbm,
    gh_ref, gl_ref, scaled_ref,
    w, hid, og, meta, gmeta, onehot, disp, wcol, acc, snd, rcv, dsl, dc, dcr, ret, lt_pad,
    load_sem, og_s, og_r, mt_s, mt_r, rs_s, rs_r, ar_s, ar_r, z_s, z_r,
):
    me_d, me_z = lax.axis_index("dp"), lax.axis_index("expert")
    levels = nd.bit_length() - 1
    rows = nd * pad
    half = rows // 2
    tok = og_ref.shape[0]
    hidden_units = w.shape[1]

    loads = []
    for e in range(experts):
        pair = (
            pltpu.make_async_copy(w_hbm.at[e], w.at[e], load_sem.at[2 * e]),
            pltpu.make_async_copy(hid_hbm.at[e], hid.at[e], load_sem.at[2 * e + 1]),
        )
        for copy in pair:
            copy.start()
        loads.append(pair)

    barrier = pltpu.get_barrier_semaphore()
    for k in range(1, nz):
        pl.semaphore_signal(barrier, inc=1, device_id=(me_d, lax.rem(me_z + k, nz)), device_id_type=MESH)
    for b in range(levels):
        pl.semaphore_signal(barrier, inc=1, device_id=(flipped(me_d, b), me_z), device_id_type=MESH)

    lt_pad[...] = jnp.full(lt_pad.shape, -1e30, F32)
    for z in range(nz):
        lt_pad[z * GROUP : z * GROUP + experts] = lt_ref[z * experts : (z + 1) * experts]
    lt = lt_pad[...]
    row = lax.broadcasted_iota(jnp.int32, lt.shape, 0)
    local = lax.rem(row, GROUP)
    eid = jnp.where(local < experts, (row // GROUP) * experts + local, -1)
    top = rt_ref.shape[0]
    chosen = jnp.zeros(lt.shape, F32)
    for k in range(top):
        chosen = jnp.where(rt_ref[k : k + 1, :] == eid, 1.0, chosen)
    raised = jnp.exp(lt - jnp.max(lt, axis=0, keepdims=True))
    probs = raised / jnp.sum(raised, axis=0, keepdims=True)
    sel = probs * chosen
    wsum = jnp.sum(sel, axis=0, keepdims=True)
    comb = sel / wsum
    t2 = lax.broadcasted_iota(jnp.int32, (tok, tok), 0)
    t1 = lax.broadcasted_iota(jnp.int32, (tok, tok), 1)
    earlier = jnp.where(t2 < t1, 1.0, 0.0).astype(BF16)
    rank = jnp.dot(chosen.astype(BF16), earlier, preferred_element_type=F32)
    place = jnp.where(chosen > 0.5, rank, -1.0)
    for z in range(nz):
        part = slice(z * GROUP, (z + 1) * GROUP)
        meta[z] = jnp.concatenate([place[part], comb[part]], axis=0).astype(BF16)

    pl.semaphore_wait(barrier, nz - 1 + levels)
    copies = []
    for k in range(1, nz):
        to = lax.rem(me_z + k, nz)
        copies.append(pltpu.make_async_remote_copy(
            src_ref=og_ref, dst_ref=og.at[me_z], send_sem=og_s.at[k - 1], recv_sem=og_r.at[k - 1],
            device_id=(me_d, to), device_id_type=MESH))
        copies.append(pltpu.make_async_remote_copy(
            src_ref=meta.at[to], dst_ref=gmeta.at[me_z], send_sem=mt_s.at[k - 1], recv_sem=mt_r.at[k - 1],
            device_id=(me_d, to), device_id_type=MESH))
    for copy in copies:
        copy.start()
    og[me_z] = og_ref[...]
    gmeta[me_z] = meta[me_z]

    at = lax.broadcasted_iota(jnp.int32, (rows, tok), 0)
    position, inside = at // pad, lax.rem(at, pad)
    slot_at = []
    for stream in range(2):
        bits = stream_bits(levels, stream)
        owner = jnp.zeros_like(at)
        for k, b in enumerate(bits):
            differs = lax.rem(position // (1 << (levels - 1 - k)), 2)
            owner = owner + (1 << b) * lax.rem(differs + bit_of(me_d, b), 2)
        slot_at.append(jnp.where(inside < own, owner * own + inside, -7).astype(F32))

    def owner_of(p, bits):
        r = relative(p, bits)
        return sum((1 << b) * lax.rem(bit_of(r, b) + bit_of(me_d, b), 2) for b in range(levels))

    for copy in copies:
        copy.wait()

    def rs_copy(e, level):
        bits = stream_bits(levels, e)
        size = rows >> (level + 1)
        start = rows - (rows >> level)
        return pltpu.make_async_remote_copy(
            src_ref=snd.at[e, pl.ds(start, size)], dst_ref=rcv.at[e, pl.ds(start, size)],
            send_sem=rs_s.at[e * levels + level], recv_sem=rs_r.at[e * levels + level],
            device_id=(flipped(me_d, bits[level]), me_z), device_id_type=MESH)

    def compute(e):
        bits = stream_bits(levels, e)
        slots = slot_at[e % 2]
        wcol[e] = jnp.zeros((rows, tok), F32)

        def dispatch(s):
            told = gmeta[s].astype(F32)
            place_row, comb_row = told[e : e + 1], told[GROUP + e : GROUP + e + 1]
            offset = s * cap if isinstance(s, int) else (s * cap).astype(F32)
            absolute = jnp.where(place_row >= 0.0, place_row + offset, -1.0)
            hit = slots == absolute
            lanes = pl.ds(s * tok if isinstance(s, int) else pl.multiple_of(s * tok, tok), tok)
            onehot[e, :, lanes] = jnp.where(hit, 1.0, 0.0).astype(BF16)
            wcol[e] += jnp.where(hit, comb_row, 0.0)

        if nz <= 8:
            for s in range(nz):
                dispatch(s)
        else:
            @pl.loop(0, nz)
            def _(s):
                dispatch(s)

        weight = jnp.sum(wcol[e], axis=1, keepdims=True)
        wcol[e] = jnp.broadcast_to(weight, (rows, tok))
        cols = og.shape[2]
        d = jnp.dot(onehot[e], og[...].reshape(nz * tok, cols), preferred_element_type=F32)
        disp[...] = d.astype(BF16)
        scaled = (weight * d).astype(BF16)
        for p in range(nd):
            scaled_ref[e, owner_of(p, bits)] = scaled[p * pad : (p + 1) * pad]
        for copy in loads[e]:
            copy.wait()
        dsl[...] = jnp.zeros(dsl.shape, F32)

        @pl.loop(0, hidden_units // ft)
        def _(i):
            part = pl.ds(pl.multiple_of(i * ft, ft), ft)
            u = lax.dot_general(disp[...], w[e, part, :], (((1,), (1,)), ((), ())), preferred_element_type=F32)
            acc[e, :, part] = u[:half]
            snd[e, 0:half, part] = u[half:].astype(BF16)
            for p in range(nd):
                prod = u[p * pad : (p + 1) * pad] * hid[e, owner_of(p, bits), :, part].astype(F32)
                total = prod[:, 0:128]
                for c in range(128, ft, 128):
                    total = total + prod[:, c : c + 128]
                dsl[p * pad : (p + 1) * pad, :] += total

        rs_copy(e, 0).start()
        line = jnp.sum(jnp.transpose(dsl[...]), axis=0, keepdims=True)
        high = line.astype(BF16).astype(F32)
        mid = (line - high).astype(BF16).astype(F32)
        low = line - high - mid
        which = lax.broadcasted_iota(jnp.int32, (16, rows), 0)
        three = jnp.where(which == 0, high, jnp.where(which == 1, mid, jnp.where(which == 2, low, 0.0))).astype(BF16)
        back = jnp.dot(three, onehot[e], preferred_element_type=F32)
        back = jnp.sum(back, axis=0, keepdims=True)
        for s in range(nz):
            dc[0, s, e : e + 1, :] = back[:, s * tok : (s + 1) * tok]

    def advance(e, level):
        copy = rs_copy(e, level)
        copy.wait()
        size = rows >> (level + 1)
        start = rows - (rows >> level)
        if level < levels - 1:
            keep = size // 2
            snd[e, start + size : start + size + keep] = (
                acc[e, keep:size] + rcv[e, start + keep : start + size].astype(F32)).astype(BF16)
            rs_copy(e, level + 1).start()
            acc[e, 0:keep] += rcv[e, start : start + keep].astype(F32)
        else:
            total = acc[e, 0:size] + rcv[e, start : start + size].astype(F32)
            gh_ref[:, e, :] = (wcol[e, 0:size, 0:1] * total).astype(BF16)[:own]

    def ar_copy(level):
        return pltpu.make_async_remote_copy(
            src_ref=dc.at[level], dst_ref=dcr.at[level], send_sem=ar_s.at[level], recv_sem=ar_r.at[level],
            device_id=(flipped(me_d, level), me_z), device_id_type=MESH)

    dc[0] = jnp.zeros(dc.shape[1:], F32)
    compute(0)
    for e in range(1, experts):
        compute(e)
        advance(e - 1, 0)

    def ar_step(level):
        ar_copy(level).wait()
        dc[level + 1] = dc[level] + dcr[level]

    ar_copy(0).start()
    advance(experts - 1, 0)
    for level in range(levels):
        ar_step(level)
        if level + 1 < levels:
            ar_copy(level + 1).start()
    returns = []
    for k in range(1, nz):
        to = lax.rem(me_z + k, nz)
        returns.append(pltpu.make_async_remote_copy(
            src_ref=dc.at[levels, to], dst_ref=ret.at[me_z], send_sem=z_s.at[k - 1], recv_sem=z_r.at[k - 1],
            device_id=(me_d, to), device_id_type=MESH))
    for copy in returns:
        copy.start()
    ret[me_z] = dc[levels, me_z]

    for level in range(1, levels):
        for e in range(experts):
            advance(e, level)

    for copy in returns:
        copy.wait()
    dcomb = ret[...].reshape(nz * GROUP, tok)
    dsel = (dcomb - jnp.sum(comb * dcomb, axis=0, keepdims=True)) / wsum
    spread = jnp.where(chosen > 0.5, dsel, 0.0)
    out = probs * (spread - jnp.sum(sel * spread, axis=0, keepdims=True))
    for z in range(nz):
        gl_ref[z * experts : (z + 1) * experts] = out[z * GROUP : z * GROUP + experts]


def grad_kernel(hid_ref, scaled_ref, gh_ref, gl_ref, gd_out, gh_out, gl_out):
    @pl.when(pl.program_id(1) == 0)
    def _():
        gh_out[...] = gh_ref[...]
        gl_out[...] = gl_ref[...]

    h = hid_ref[0].reshape(-1, hid_ref.shape[-1])
    x = scaled_ref[0].reshape(-1, scaled_ref.shape[-1])
    gd_out[0] = lax.dot_general(h, x, (((0,), (0,)), ((), ())), preferred_element_type=F32).astype(BF16)


def per_device(out_grad, logits, routes, hidden, w_down):
    tok, cols = out_grad.shape
    experts, slot_count, units = hidden.shape
    nz, nd = lax.axis_size("expert"), lax.axis_size("dp")
    cap, own = slot_count // nz, slot_count // nd
    pad = -(-own // 16) * 16
    rows, levels = nd * pad, nd.bit_length() - 1
    ft = next(f for f in (512, 384, 256, 128) if units % f == 0)

    hid = hidden.reshape(experts, nd, own, units)
    if pad != own:
        hid = jnp.pad(hid, ((0, 0), (0, 0), (0, pad - own), (0, 0)))
    vmem, hbm = pl.BlockSpec(memory_space=pltpu.VMEM), pl.BlockSpec(memory_space=pl.ANY)
    dma = lambda n: pltpu.SemaphoreType.DMA((n,))
    gh, gl, scaled = pl.pallas_call(
        functools.partial(kernel, nz, nd, own, pad, cap, experts, ft),
        out_shape=(
            jax.ShapeDtypeStruct((own, experts, units), BF16),
            jax.ShapeDtypeStruct((nz * experts, tok), F32),
            jax.ShapeDtypeStruct((experts, nd, pad, cols), BF16),
        ),
        in_specs=[vmem, vmem, vmem, hbm, hbm],
        out_specs=(vmem, vmem, vmem),
        scratch_shapes=[
            pltpu.VMEM((experts, units, cols), BF16),
            pltpu.VMEM((experts, nd, pad, units), BF16),
            pltpu.VMEM((nz, tok, cols), BF16),
            pltpu.VMEM((nz, 2 * GROUP, tok), BF16),
            pltpu.VMEM((nz, 2 * GROUP, tok), BF16),
            pltpu.VMEM((experts, rows, nz * tok), BF16),
            pltpu.VMEM((rows, cols), BF16),
            pltpu.VMEM((experts, rows, tok), F32),
            pltpu.VMEM((experts, rows // 2, units), F32),
            pltpu.VMEM((experts, rows, units), BF16),
            pltpu.VMEM((experts, rows, units), BF16),
            pltpu.VMEM((rows, 128), F32),
            pltpu.VMEM((levels + 1, nz, GROUP, tok), F32),
            pltpu.VMEM((levels, nz, GROUP, tok), F32),
            pltpu.VMEM((nz, GROUP, tok), F32),
            pltpu.VMEM((nz * GROUP, tok), F32),
            dma(2 * experts), dma(nz - 1), dma(nz - 1), dma(nz - 1), dma(nz - 1),
            dma(experts * levels), dma(experts * levels), dma(levels), dma(levels), dma(nz - 1), dma(nz - 1),
        ],
        compiler_params=pltpu.CompilerParams(
            collective_id=0, has_side_effects=True, vmem_limit_bytes=60 * 1024 * 1024),
    )(out_grad, logits.T, routes.T, hid, w_down)

    gt = next(f for f in (768, 512, 384, 256, 128) if units % f == 0)
    grad_down, grad_hidden, grad_logits = pl.pallas_call(
        grad_kernel,
        grid=(experts, units // gt),
        in_specs=[
            pl.BlockSpec((1, nd, pad, gt), lambda e, i: (e, 0, 0, i)),
            pl.BlockSpec((1, nd, pad, cols), lambda e, i: (e, 0, 0, 0)),
            pl.BlockSpec((own // experts, experts, units), lambda e, i: (e, 0, 0)),
            pl.BlockSpec(gl.shape, lambda e, i: (0, 0)),
        ],
        out_specs=(
            pl.BlockSpec((1, gt, cols), lambda e, i: (e, i, 0)),
            pl.BlockSpec((own // experts, experts, units), lambda e, i: (e, 0, 0)),
            pl.BlockSpec(gl.shape, lambda e, i: (0, 0)),
        ),
        out_shape=(
            jax.ShapeDtypeStruct((experts, units, cols), BF16),
            jax.ShapeDtypeStruct((own, experts, units), BF16),
            jax.ShapeDtypeStruct(gl.shape, F32),
        ),
        compiler_params=pltpu.CompilerParams(vmem_limit_bytes=60 * 1024 * 1024),
    )(hid, scaled, gh, gl)
    return grad_down, grad_hidden, grad_logits.T


def solution(mesh):
    return jax.shard_map(
        per_device,
        mesh=mesh,
        in_specs=(
            P("expert", "dp"),
            P("expert", None),
            P("expert", None),
            P("expert", None, None),
            P("expert", None, "dp"),
        ),
        out_specs=(P("expert", None, "dp"), P("dp", "expert", None), P("expert", None)),
        check_vma=False,
    )
```

```python
import functools

import jax
import jax.numpy as jnp
from jax import lax
from jax.experimental import pallas as pl
from jax.experimental.pallas import tpu as pltpu
from jax.sharding import PartitionSpec as P

MESH = pl.DeviceIdType.MESH
F32, BF16 = jnp.float32, jnp.bfloat16
GROUP = 8


def bit_of(value, b):
    return lax.rem(value // (1 << b), 2) if not isinstance(value, int) else (value >> b) & 1


def flipped(value, b):
    return value + (1 << b) * (1 - 2 * bit_of(value, b))


def stream_bits(levels, expert):
    rest = list(range(1, levels))
    return [0] + (rest if expert % 2 == 0 else rest[::-1])


def relative(position, bits):
    levels = len(bits)
    return sum(((position >> (levels - 1 - k)) & 1) << b for k, b in enumerate(bits))


def kernel(
    nz, nd, own, pad, cap, experts, ft,
    og_ref, lt_ref, rt_ref, hid_hbm, w_hbm,
    gh_ref, gl_ref, scaled_ref,
    w, hid, og, meta, gmeta, onehot, disp, wcol, acc, snd, rcv, dsl, dc, dcr, ret, lt_pad,
    load_sem, og_s, og_r, mt_s, mt_r, rs_s, rs_r, ar_s, ar_r, z_s, z_r,
):
    me_d, me_z = lax.axis_index("dp"), lax.axis_index("expert")
    levels = nd.bit_length() - 1
    rows = nd * pad
    half = rows // 2
    tok = og_ref.shape[0]
    hidden_units = w.shape[1]

    loads = []
    for e in range(experts):
        pair = (
            pltpu.make_async_copy(w_hbm.at[e], w.at[e], load_sem.at[2 * e]),
            pltpu.make_async_copy(hid_hbm.at[e], hid.at[e], load_sem.at[2 * e + 1]),
        )
        for copy in pair:
            copy.start()
        loads.append(pair)

    barrier = pltpu.get_barrier_semaphore()
    for k in range(1, nz):
        pl.semaphore_signal(barrier, inc=1, device_id=(me_d, lax.rem(me_z + k, nz)), device_id_type=MESH)
    for b in range(levels):
        pl.semaphore_signal(barrier, inc=1, device_id=(flipped(me_d, b), me_z), device_id_type=MESH)

    lt_pad[...] = jnp.full(lt_pad.shape, -1e30, F32)
    for z in range(nz):
        lt_pad[z * GROUP : z * GROUP + experts] = lt_ref[z * experts : (z + 1) * experts]
    lt = lt_pad[...]
    row = lax.broadcasted_iota(jnp.int32, lt.shape, 0)
    local = lax.rem(row, GROUP)
    eid = jnp.where(local < experts, (row // GROUP) * experts + local, -1)
    top = rt_ref.shape[0]
    chosen = jnp.zeros(lt.shape, F32)
    for k in range(top):
        chosen = jnp.where(rt_ref[k : k + 1, :] == eid, 1.0, chosen)
    raised = jnp.exp(lt - jnp.max(lt, axis=0, keepdims=True))
    probs = raised / jnp.sum(raised, axis=0, keepdims=True)
    sel = probs * chosen
    wsum = jnp.sum(sel, axis=0, keepdims=True)
    comb = sel / wsum
    t2 = lax.broadcasted_iota(jnp.int32, (tok, tok), 0)
    t1 = lax.broadcasted_iota(jnp.int32, (tok, tok), 1)
    earlier = jnp.where(t2 < t1, 1.0, 0.0).astype(BF16)
    rank = jnp.dot(chosen.astype(BF16), earlier, preferred_element_type=F32)
    place = jnp.where(chosen > 0.5, rank, -1.0)
    for z in range(nz):
        part = slice(z * GROUP, (z + 1) * GROUP)
        meta[z] = jnp.concatenate([place[part], comb[part]], axis=0).astype(BF16)

    pl.semaphore_wait(barrier, nz - 1 + levels)
    copies = []
    for k in range(1, nz):
        to = lax.rem(me_z + k, nz)
        copies.append(pltpu.make_async_remote_copy(
            src_ref=og_ref, dst_ref=og.at[me_z], send_sem=og_s.at[k - 1], recv_sem=og_r.at[k - 1],
            device_id=(me_d, to), device_id_type=MESH))
        copies.append(pltpu.make_async_remote_copy(
            src_ref=meta.at[to], dst_ref=gmeta.at[me_z], send_sem=mt_s.at[k - 1], recv_sem=mt_r.at[k - 1],
            device_id=(me_d, to), device_id_type=MESH))
    for copy in copies:
        copy.start()
    og[me_z] = og_ref[...]
    gmeta[me_z] = meta[me_z]

    at = lax.broadcasted_iota(jnp.int32, (rows, tok), 0)
    position, inside = at // pad, lax.rem(at, pad)
    slot_at = []
    for stream in range(2):
        bits = stream_bits(levels, stream)
        owner = jnp.zeros_like(at)
        for k, b in enumerate(bits):
            differs = lax.rem(position // (1 << (levels - 1 - k)), 2)
            owner = owner + (1 << b) * lax.rem(differs + bit_of(me_d, b), 2)
        slot_at.append(jnp.where(inside < own, owner * own + inside, -7).astype(F32))

    def owner_of(p, bits):
        r = relative(p, bits)
        return sum((1 << b) * lax.rem(bit_of(r, b) + bit_of(me_d, b), 2) for b in range(levels))

    for copy in copies:
        copy.wait()

    def rs_copy(e, level):
        bits = stream_bits(levels, e)
        size = rows >> (level + 1)
        start = rows - (rows >> level)
        return pltpu.make_async_remote_copy(
            src_ref=snd.at[e, pl.ds(start, size)], dst_ref=rcv.at[e, pl.ds(start, size)],
            send_sem=rs_s.at[e * levels + level], recv_sem=rs_r.at[e * levels + level],
            device_id=(flipped(me_d, bits[level]), me_z), device_id_type=MESH)

    def compute(e):
        bits = stream_bits(levels, e)
        slots = slot_at[e % 2]
        wcol[e] = jnp.zeros((rows, tok), F32)

        def dispatch(s):
            told = gmeta[s].astype(F32)
            place_row, comb_row = told[e : e + 1], told[GROUP + e : GROUP + e + 1]
            offset = s * cap if isinstance(s, int) else (s * cap).astype(F32)
            absolute = jnp.where(place_row >= 0.0, place_row + offset, -1.0)
            hit = slots == absolute
            lanes = pl.ds(s * tok if isinstance(s, int) else pl.multiple_of(s * tok, tok), tok)
            onehot[e, :, lanes] = jnp.where(hit, 1.0, 0.0).astype(BF16)
            wcol[e] += jnp.where(hit, comb_row, 0.0)

        if nz <= 8:
            for s in range(nz):
                dispatch(s)
        else:
            @pl.loop(0, nz)
            def _(s):
                dispatch(s)

        weight = jnp.sum(wcol[e], axis=1, keepdims=True)
        wcol[e] = jnp.broadcast_to(weight, (rows, tok))
        cols = og.shape[2]
        d = jnp.dot(onehot[e], og[...].reshape(nz * tok, cols), preferred_element_type=F32)
        disp[...] = d.astype(BF16)
        scaled = (weight * d).astype(BF16)
        for p in range(nd):
            scaled_ref[e, owner_of(p, bits)] = scaled[p * pad : (p + 1) * pad]
        for copy in loads[e]:
            copy.wait()
        dsl[...] = jnp.zeros(dsl.shape, F32)

        @pl.loop(0, hidden_units // ft)
        def _(i):
            part = pl.ds(pl.multiple_of(i * ft, ft), ft)
            u = lax.dot_general(disp[...], w[e, part, :], (((1,), (1,)), ((), ())), preferred_element_type=F32)
            acc[e, :, part] = u[:half]
            snd[e, 0:half, part] = u[half:].astype(BF16)
            for p in range(nd):
                prod = u[p * pad : (p + 1) * pad] * hid[e, owner_of(p, bits), :, part].astype(F32)
                total = prod[:, 0:128]
                for c in range(128, ft, 128):
                    total = total + prod[:, c : c + 128]
                dsl[p * pad : (p + 1) * pad, :] += total

        rs_copy(e, 0).start()
        line = jnp.sum(jnp.transpose(dsl[...]), axis=0, keepdims=True)
        high = line.astype(BF16).astype(F32)
        mid = (line - high).astype(BF16).astype(F32)
        low = line - high - mid
        which = lax.broadcasted_iota(jnp.int32, (16, rows), 0)
        three = jnp.where(which == 0, high, jnp.where(which == 1, mid, jnp.where(which == 2, low, 0.0))).astype(BF16)
        back = jnp.dot(three, onehot[e], preferred_element_type=F32)
        back = jnp.sum(back, axis=0, keepdims=True)
        for s in range(nz):
            dc[0, s, e : e + 1, :] = back[:, s * tok : (s + 1) * tok]

    def advance(e, level):
        copy = rs_copy(e, level)
        copy.wait()
        size = rows >> (level + 1)
        start = rows - (rows >> level)
        if level < levels - 1:
            keep = size // 2
            snd[e, start + size : start + size + keep] = (
                acc[e, keep:size] + rcv[e, start + keep : start + size].astype(F32)).astype(BF16)
            rs_copy(e, level + 1).start()
            acc[e, 0:keep] += rcv[e, start : start + keep].astype(F32)
        else:
            total = acc[e, 0:size] + rcv[e, start : start + size].astype(F32)
            gh_ref[:, e, :] = (wcol[e, 0:size, 0:1] * total).astype(BF16)[:own]

    def ar_copy(level):
        return pltpu.make_async_remote_copy(
            src_ref=dc.at[level], dst_ref=dcr.at[level], send_sem=ar_s.at[level], recv_sem=ar_r.at[level],
            device_id=(flipped(me_d, level), me_z), device_id_type=MESH)

    dc[0] = jnp.zeros(dc.shape[1:], F32)
    compute(0)
    for e in range(1, experts):
        compute(e)
        advance(e - 1, 0)

    def ar_step(level):
        ar_copy(level).wait()
        dc[level + 1] = dc[level] + dcr[level]

    ar_copy(0).start()
    advance(experts - 1, 0)
    for level in range(levels):
        ar_step(level)
        if level + 1 < levels:
            ar_copy(level + 1).start()
    returns = []
    for k in range(1, nz):
        to = lax.rem(me_z + k, nz)
        returns.append(pltpu.make_async_remote_copy(
            src_ref=dc.at[levels, to], dst_ref=ret.at[me_z], send_sem=z_s.at[k - 1], recv_sem=z_r.at[k - 1],
            device_id=(me_d, to), device_id_type=MESH))
    for copy in returns:
        copy.start()
    ret[me_z] = dc[levels, me_z]

    for level in range(1, levels):
        for e in range(experts):
            advance(e, level)

    for copy in returns:
        copy.wait()
    dcomb = ret[...].reshape(nz * GROUP, tok)
    dsel = (dcomb - jnp.sum(comb * dcomb, axis=0, keepdims=True)) / wsum
    spread = jnp.where(chosen > 0.5, dsel, 0.0)
    out = probs * (spread - jnp.sum(sel * spread, axis=0, keepdims=True))
    for z in range(nz):
        gl_ref[z * experts : (z + 1) * experts] = out[z * GROUP : z * GROUP + experts]


def grad_kernel(hid_ref, scaled_ref, gh_ref, gl_ref, gd_out, gh_out, gl_out):
    @pl.when(pl.program_id(1) == 0)
    def _():
        gh_out[...] = gh_ref[...]
        gl_out[...] = gl_ref[...]

    h = hid_ref[0].reshape(-1, hid_ref.shape[-1])
    x = scaled_ref[0].reshape(-1, scaled_ref.shape[-1])
    gd_out[0] = lax.dot_general(h, x, (((0,), (0,)), ((), ())), preferred_element_type=F32).astype(BF16)


def per_device(out_grad, logits, routes, hidden, w_down):
    tok, cols = out_grad.shape
    experts, slot_count, units = hidden.shape
    nz, nd = lax.axis_size("expert"), lax.axis_size("dp")
    cap, own = slot_count // nz, slot_count // nd
    pad = -(-own // 16) * 16
    rows, levels = nd * pad, nd.bit_length() - 1
    ft = next(f for f in (512, 384, 256, 128) if units % f == 0)

    hid = hidden.reshape(experts, nd, own, units)
    if pad != own:
        hid = jnp.pad(hid, ((0, 0), (0, 0), (0, pad - own), (0, 0)))
    vmem, hbm = pl.BlockSpec(memory_space=pltpu.VMEM), pl.BlockSpec(memory_space=pl.ANY)
    far = pl.BlockSpec(memory_space=pltpu.HBM)
    dma = lambda n: pltpu.SemaphoreType.DMA((n,))
    gh, gl, scaled = pl.pallas_call(
        functools.partial(kernel, nz, nd, own, pad, cap, experts, ft),
        out_shape=(
            jax.ShapeDtypeStruct((own, experts, units), BF16),
            jax.ShapeDtypeStruct((nz * experts, tok), F32),
            jax.ShapeDtypeStruct((experts, nd, pad, cols), BF16),
        ),
        in_specs=[vmem, vmem, vmem, far, far],
        out_specs=(vmem, vmem, vmem),
        scratch_shapes=[
            pltpu.VMEM((experts, units, cols), BF16),
            pltpu.VMEM((experts, nd, pad, units), BF16),
            pltpu.VMEM((nz, tok, cols), BF16),
            pltpu.VMEM((nz, 2 * GROUP, tok), BF16),
            pltpu.VMEM((nz, 2 * GROUP, tok), BF16),
            pltpu.VMEM((experts, rows, nz * tok), BF16),
            pltpu.VMEM((rows, cols), BF16),
            pltpu.VMEM((experts, rows, tok), F32),
            pltpu.VMEM((experts, rows // 2, units), F32),
            pltpu.VMEM((experts, rows, units), BF16),
            pltpu.VMEM((experts, rows, units), BF16),
            pltpu.VMEM((rows, 128), F32),
            pltpu.VMEM((levels + 1, nz, GROUP, tok), F32),
            pltpu.VMEM((levels, nz, GROUP, tok), F32),
            pltpu.VMEM((nz, GROUP, tok), F32),
            pltpu.VMEM((nz * GROUP, tok), F32),
            dma(2 * experts), dma(nz - 1), dma(nz - 1), dma(nz - 1), dma(nz - 1),
            dma(experts * levels), dma(experts * levels), dma(levels), dma(levels), dma(nz - 1), dma(nz - 1),
        ],
        compiler_params=pltpu.CompilerParams(
            collective_id=0, has_side_effects=True, vmem_limit_bytes=(44 if nz * tok <= 1024 else 60) * 1024 * 1024),
    )(out_grad, logits.T, routes.T, hid, w_down)

    gt = next(f for f in (768, 512, 384, 256, 128) if units % f == 0)
    grad_down, grad_hidden, grad_logits = pl.pallas_call(
        grad_kernel,
        grid=(experts, units // gt),
        in_specs=[
            pl.BlockSpec((1, nd, pad, gt), lambda e, i: (e, 0, 0, i)),
            pl.BlockSpec((1, nd, pad, cols), lambda e, i: (e, 0, 0, 0)),
            pl.BlockSpec((own // experts, experts, units), lambda e, i: (e, 0, 0)),
            pl.BlockSpec(gl.shape, lambda e, i: (0, 0)),
        ],
        out_specs=(
            pl.BlockSpec((1, gt, cols), lambda e, i: (e, i, 0)),
            pl.BlockSpec((own // experts, experts, units), lambda e, i: (e, 0, 0)),
            pl.BlockSpec(gl.shape, lambda e, i: (0, 0)),
        ),
        out_shape=(
            jax.ShapeDtypeStruct((experts, units, cols), BF16),
            jax.ShapeDtypeStruct((own, experts, units), BF16),
            jax.ShapeDtypeStruct(gl.shape, F32),
        ),
        compiler_params=pltpu.CompilerParams(vmem_limit_bytes=16 * 1024 * 1024),
    )(hid, scaled, gh, gl)
    return grad_down, grad_hidden, grad_logits.T


def solution(mesh):
    return jax.shard_map(
        per_device,
        mesh=mesh,
        in_specs=(
            P("expert", "dp"),
            P("expert", None),
            P("expert", None),
            P("expert", None, None),
            P("expert", None, "dp"),
        ),
        out_specs=(P("expert", None, "dp"), P("dp", "expert", None), P("expert", None)),
        check_vma=False,
    )
```
